32 devices in a mesh: groups: 2 (over y), row: 4 (over z), col: 2 (over x), rep: 2 (over core).
Axes of the slice: x: 2, y: 2, z: 4, core: 2. Of those that a mesh axis runs over, the one named last changes fastest.
Arguments:
- basis_values: bfloat16 [9216, 2048], P('row', ('col', 'rep')), may hold values from -6 to 6
- orbital_values: bfloat16 [4096, 128], P(('groups', 'col', 'rep')), parts along dimension 0, may hold values from -6 to 6
- z_tiles: bfloat16 [64, 128, 128], P('row'), may hold values from -0.00036621094 to 0.00036621094
- tile_pairs: int32 [64, 2], P('row'), may hold values from 0 to 15, as said below
Outputs:
- exchange: float32 [18432, 4, 2304], P(('groups', 'row'), ('col', 'rep')), parts along dimension 0
The draws below stay inside these ranges and needn't reach their ends.
There are 2 independent parts, one for each index of `groups`. The reference program is written for one: setup_inputs(seed, part) draws one part's arguments, and reference() takes and returns one part's arrays. A program takes and returns all parts, laid end to end along the dimension named above; an argument that names none is the same for every part. Nothing has to cross between parts.
Inputs may be any that keep to these rules, and one draw needn't show every extreme that they name: `tile_pairs`: the column tile is the row tile plus 0 to 2, modulo 16; each tile is the row tile of exactly 4 pairs; a pair may repeat.
All inputs are finite; a program needn't handle non-finite values.
Results may differ from the reference program's by a relative error of at most 0.0075.
Values may be sent and summed in bfloat16 or wider, within the bound.
A program may use at most 192 MiB of HBM per device.

```python
import jax
import jax.numpy as jnp
from jax import lax

NB = 9216
NO = 128
TP = 128
NT = 16
BANDW = 2
P_SIZE = 2048
NPAIR = 64
N_ROW = 4
N_COL = 2
N_REP = 2


def draw_tile_pairs(key, part):
    key = jax.random.fold_in(key, 7)
    order_key, offset_key = jax.random.split(key)
    first_tile = jax.random.permutation(order_key, NPAIR) % NT
    offsets = jax.random.randint(offset_key, (NPAIR,), 0, BANDW + 1)
    second_tile = (first_tile + offsets) % NT
    return jnp.stack([first_tile, second_tile], axis=1).astype(jnp.int32)


def steps_of(own_key, dims, cuts, smallest, largest):
    factor_of = 1.0
    for position, blocks in cuts:
        steps = jax.random.uniform(jax.random.fold_in(jax.random.fold_in(own_key, 6), position), (blocks,), jnp.float32, smallest / len(cuts), largest / len(cuts))
        factor_of = factor_of * jnp.repeat(jnp.exp(steps), dims[position] // blocks).reshape((-1,) + (1,) * (len(dims) - 1 - position))
    return factor_of


def bell_draw(stream_key, extent, spread, most, pieces=(), held_as=jnp.bfloat16):
    gain = steps_of(stream_key, extent, pieces, -0.22, 0.18) if pieces else 1.0
    entries = jax.random.normal(stream_key, extent, jnp.float32) * spread * gain
    return jnp.minimum(jnp.maximum(entries, -most), most).astype(held_as)


def setup_inputs(seed: int = 0, part: int = 0) -> dict:
    seeds = jax.random.split(jax.random.key(seed), 5)
    part_splits = jax.random.split(jax.random.fold_in(seeds[4], part), 5)
    basis_values = bell_draw(seeds[0], (NB, P_SIZE), 1.0, 6.0, ((0, 4), (1, 4)))
    orbital_values = bell_draw(part_splits[1], (P_SIZE, NO), 1.0, 6.0, ((0, 4),))
    z_tiles = bell_draw(seeds[2], (NPAIR, TP, TP), (8 * P_SIZE * TP * NO) ** -0.5, 0.00036621094, ((0, 4),))
    tile_pairs = draw_tile_pairs(jax.random.fold_in(seeds[4], 71), part)
    return {"basis_values": basis_values, "orbital_values": orbital_values, "z_tiles": z_tiles, "tile_pairs": tile_pairs}


def reference(basis_values, orbital_values, z_tiles, tile_pairs):
    basis_tiles = basis_values.reshape(NB, NT, TP)
    orbital_tiles = orbital_values.reshape(NT, TP, NO)

    def add_pair(running, scan_item):
        tile_block, pair_row = scan_item
        first_tile = pair_row[0].astype(jnp.int32)
        second_tile = pair_row[1].astype(jnp.int32)
        orbital_first = lax.dynamic_index_in_dim(orbital_tiles, first_tile, 0, keepdims=False)
        orbital_second = lax.dynamic_index_in_dim(orbital_tiles, second_tile, 0, keepdims=False)
        intersection = jnp.dot(orbital_first, orbital_second.T, preferred_element_type=jnp.float32)
        weights = (tile_block.astype(jnp.float32) * intersection).astype(jnp.bfloat16)
        basis_first = lax.dynamic_index_in_dim(basis_tiles, first_tile, 1, keepdims=False)
        basis_second = lax.dynamic_index_in_dim(basis_tiles, second_tile, 1, keepdims=False)
        to_second = jnp.dot(basis_first, weights, preferred_element_type=jnp.float32)
        to_first = jnp.dot(basis_second, weights.T, preferred_element_type=jnp.float32)
        running = running.at[:, second_tile].add(to_second)
        running = running.at[:, first_tile].add(to_first)
        return running, None

    zero_mix = jnp.zeros((NB, NT, TP), jnp.float32)
    running, _ = lax.scan(add_pair, zero_mix, (z_tiles, tile_pairs))
    mixed_rows = running.reshape(NB, NT * TP).astype(jnp.bfloat16)
    product = jnp.dot(mixed_rows, basis_values.T, preferred_element_type=jnp.float32)
    col_groups = N_COL * N_REP
    slice_count = NB // (N_ROW * col_groups)
    arranged = product.reshape(NB, N_ROW, col_groups, slice_count).transpose(0, 2, 1, 3)
    return arranged.reshape(NB, col_groups, N_ROW * slice_count)
```

```python
import functools

import jax
import jax.numpy as jnp
from jax import lax
from jax.experimental import pallas as pl
from jax.experimental.pallas import tpu as pltpu
from jax.sharding import PartitionSpec as P

MESH = pl.DeviceIdType.MESH
BAND = 3


def gather_kernel(dims, basis, orb, z, pairs, a_all, cols, orb_all, z_all, pairs_all,
                  loc_sem, xs_sem, xr_sem, os_sem, or_sem, zs_sem, zo_sem, zr_sem,
                  ys_sem, yr_sem, ts_sem, to_sem, tr_sem, ps_sem, po_sem, pr_sem,
                  ds_sem, dr_sem):
    G, R, X, K = dims
    C = X * K
    width = basis.shape[2]
    half = width // G
    n_pair = z.shape[0]
    part = z.shape[1] // C
    g = lax.axis_index("groups")
    r = lax.axis_index("row")
    x = lax.axis_index("col")
    k = lax.axis_index("rep")
    c = x * K + k

    def col_of(dx, dk):
        return lax.rem(x + dx, X) * K + lax.rem(k + dk, K)

    def dev(dg=0, row=None, dx=0, dk=0):
        return (lax.rem(g + dg, G), r if row is None else row, lax.rem(x + dx, X), lax.rem(k + dk, K))

    def remote(src, dst, send, recv, device):
        return pltpu.make_async_remote_copy(src_ref=src, dst_ref=dst, send_sem=send, recv_sem=recv,
                                            device_id=device, device_id_type=MESH)

    others = [(dx, dk) for dx in range(X) for dk in range(K) if dx or dk]
    barrier = pltpu.get_barrier_semaphore()
    for dx, dk in others:
        pl.semaphore_signal(barrier, inc=1, device_id=dev(dx=dx, dk=dk), device_id_type=MESH)
    for dr in (1, R - 1):
        pl.semaphore_signal(barrier, inc=1, device_id=dev(row=lax.rem(r + dr, R)), device_id_type=MESH)
    for dg in range(1, G):
        pl.semaphore_signal(barrier, inc=1, device_id=dev(dg=dg), device_id_type=MESH)
    pl.semaphore_wait(barrier, len(others) + 2 + G - 1)

    def lanes(point_block):
        return pl.ds(pl.multiple_of(point_block * width, 128), width)

    def half_lanes(point_block, group):
        return pl.ds(pl.multiple_of(point_block * width + group * half, 128), half)

    def tile_rows(block):
        return z_all.at[pl.ds(block * n_pair, n_pair), pl.ds(pl.multiple_of(c * part, 16), part), :]

    own_rows = z.at[:, pl.ds(pl.multiple_of(c * part, 16), part), :]

    def up():
        return dev(row=r + 1)

    def down():
        return dev(row=r - 1)

    def own_tiles(way, to):
        return (remote(own_rows, tile_rows(r), to_sem.at[way], tr_sem.at[r], to),
                remote(pairs, pairs_all.at[r], po_sem.at[way], pr_sem.at[r], to))

    def pass_tiles(block, to):
        return (remote(tile_rows(block), tile_rows(block), ts_sem.at[block], tr_sem.at[block], to),
                remote(pairs_all.at[block], pairs_all.at[block], ps_sem.at[block], pr_sem.at[block], to))

    def piece(block, point_block, group):
        return cols.at[block, :, half_lanes(point_block, group)]

    def own_piece(point_block, way, to, local):
        if local:
            src = basis.at[c, :, pl.ds(pl.multiple_of(g * half, 128), half)]
        else:
            src = a_all.at[c, :, half_lanes(point_block, g)]
        return remote(src, piece(r, point_block, g), zo_sem.at[way, point_block],
                      zr_sem.at[r, point_block], to)

    def pass_piece(block, point_block, to):
        ref = piece(block, point_block, g)
        return remote(ref, ref, zs_sem.at[block, point_block], zr_sem.at[block, point_block], to)

    def swap_piece(block, point_block, dg):
        ref = piece(block, point_block, g)
        return remote(ref, ref, ys_sem.at[dg - 1, block, point_block],
                      yr_sem.at[dg - 1, block, point_block], dev(dg=dg))

    def got_piece(block, point_block, dg):
        ref = piece(block, point_block, lax.rem(g + G - dg, G))
        return remote(ref, ref, ys_sem.at[dg - 1, block, point_block],
                      yr_sem.at[dg - 1, block, point_block], dev(dg=dg))

    def each(action, items):
        for item in items:
            getattr(item, action)()

    def both_ways(do):
        pl.when(r + 1 < R)(lambda: do(0, up()))
        pl.when(r > 0)(lambda: do(1, down()))

    def start_own(point_block, local=False):
        both_ways(lambda way, to: own_piece(point_block, way, to, local).start())

    both_ways(lambda way, to: each("start", own_tiles(way, to)))
    start_own(c, True)

    def to_core(dk, s):
        ref = a_all.at[s, :, lanes(c)]
        return remote(basis.at[s], ref, xs_sem.at[0, dk, s], xr_sem.at[0, dk, s], dev(dk=K - dk))

    def to_chip(dx, s):
        ref = a_all.at[s, :, lanes(c)]
        return remote(basis.at[s], ref, xs_sem.at[dx, 0, s], xr_sem.at[dx, 0, s], dev(dx=X - dx))

    def from_other(dx, dk, s):
        ref = a_all.at[s, :, lanes(col_of(dx, dk))]
        return remote(ref, ref, xs_sem.at[dx, dk, s], xr_sem.at[dx, dk, s], dev(dk=1))

    def hand_on(dx, dk, s):
        ref = a_all.at[s, :, lanes(col_of(dx, 0))]
        return remote(ref, ref, xs_sem.at[dx, dk, s], xr_sem.at[dx, dk, s], dev(dk=K - dk))

    own_orb = orb_all.at[pl.ds(pl.multiple_of(c * width, 16), width), :]

    def orb_to(dx, dk):
        return remote(orb, own_orb, os_sem.at[dx, dk], or_sem.at[dx, dk], dev(dx=lax.rem(X - dx, X), dk=lax.rem(K - dk, K)))

    def orb_from(dx, dk):
        ref = orb_all.at[pl.ds(pl.multiple_of(col_of(dx, dk) * width, 16), width), :]
        return remote(ref, ref, os_sem.at[dx, dk], or_sem.at[dx, dk], dev(dk=1))

    order = [(dx, dk) for dx in range(X) for dk in range(K)]
    for ex, ek in order:
        for dk in range(1, K):
            to_core(dk, lax.rem(x + ex, X) * K + lax.rem(k + K - dk + ek, K)).start()
        for dx in range(1, X):
            to_chip(dx, lax.rem(x + X - dx + ex, X) * K + lax.rem(k + ek, K)).start()
        if ex == 0 and ek == 0:
            for dx, dk in others:
                orb_to(dx, dk).start()

    local = [
        pltpu.make_async_copy(basis, a_all.at[:, :, lanes(c)], loc_sem.at[0]),
        pltpu.make_async_copy(orb, own_orb, loc_sem.at[1]),
        pltpu.make_async_copy(own_rows, tile_rows(r), loc_sem.at[2]),
        pltpu.make_async_copy(pairs, pairs_all.at[r], loc_sem.at[3]),
    ]
    for copy in local:
        copy.start()

    for dk in range(1, K):
        from_other(0, dk, c).wait_recv()
        start_own(col_of(0, dk))

    def each_block(step, below, above):
        pl.when(r - step >= 0)(lambda: below(r - step))
        pl.when(r + step < R)(lambda: above(r + step))

    def relay_tiles(step, carry):
        def take(block, last, to):
            for t in pass_tiles(block, to):
                t.wait_recv()

            @pl.when(last)
            def _():
                for t in pass_tiles(block, to):
                    t.start()

        each_block(step, lambda b: take(b, r + 1 < R, up()), lambda b: take(b, r > 0, down()))
        return carry

    def relay(step, dxs):
        def take(block, point_block, more, to):
            pass_piece(block, point_block, to).wait_recv()
            pl.when(more)(lambda: pass_piece(block, point_block, to).start())
            for dg in range(1, G):
                swap_piece(block, point_block, dg).start()

        for dx in dxs:
            for dk in range(K):
                p = col_of(dx, dk)
                each_block(step, lambda b: take(b, p, r + 1 < R, up()), lambda b: take(b, p, r > 0, down()))

    lax.fori_loop(1, R, relay_tiles, 0)
    for copy in local[2:]:
        copy.wait()

    def all_rows(col):
        return z_all.at[:, pl.ds(pl.multiple_of(col * part, 16), part), :]

    def spread(dx, dk):
        return remote(all_rows(c), all_rows(c), ds_sem.at[dx, dk], dr_sem.at[dx, dk],
                      dev(dx=lax.rem(X - dx, X), dk=lax.rem(K - dk, K)))

    def spread_in(dx, dk):
        ref = all_rows(col_of(dx, dk))
        return remote(ref, ref, ds_sem.at[dx, dk], dr_sem.at[dx, dk], dev(dk=1))

    for dx, dk in others:
        spread(dx, dk).start()

    relay(1, [0])
    for dx in range(1, X):
        from_other(dx, 0, c).wait_recv()
        start_own(col_of(dx, 0))
    for dx in range(1, X):
        for dk in range(1, K):
            s = col_of(0, K - dk)
            from_other(dx, 0, s).wait_recv()
            hand_on(dx, dk, s).start()
    for dx in range(1, X):
        for dk in range(1, K):
            from_other(dx, dk, c).wait_recv()
            start_own(col_of(dx, dk))

    def first_part(step, carry):
        relay(step, [0])
        return carry

    def second_part(step, carry):
        relay(step, list(range(1, X)))
        return carry

    lax.fori_loop(2, R, first_part, 0)
    relay(1, list(range(1, X)))

    for dx in range(1, X):
        for ex, ek in order:
            if ex == 0 and ek < 1:
                for dk in range(1, K):
                    hand_on(dx, dk, c).start()
            elif ex:
                s = col_of(ex, ek)
                from_other(dx, 0, s).wait_recv()
                for dk in range(1, K):
                    hand_on(dx, dk, s).start()
            else:
                s = col_of(0, ek)
                for dk in range(1, K):
                    if K - dk != ek:
                        hand_on(dx, dk, s).start()

    lax.fori_loop(2, R, second_part, 0)

    for dx, dk in others:
        for ex, ek in order:
            if ex == 0 and ek == 0:
                continue
            if dk == 0 and dx:
                continue
            from_other(dx, dk, col_of(ex, ek)).wait_recv()
        orb_from(dx, dk).wait_recv()
        spread_in(dx, dk).wait_recv()
    local[0].wait()
    local[1].wait()
    own = pltpu.make_async_copy(a_all.at[c], cols.at[r], loc_sem.at[4])
    own.start()

    def finish(block, carry):
        @pl.when(block != r)
        def _():
            def one(p, inner):
                for dg in range(1, G):
                    got_piece(block, p, dg).wait_recv()
                    swap_piece(block, p, dg).wait_send()
                pl.when(jnp.logical_and(block < r, r + 1 < R))(lambda: pass_piece(block, p, up()).wait_send())
                pl.when(jnp.logical_and(block > r, r > 0))(lambda: pass_piece(block, p, down()).wait_send())
                return inner

            lax.fori_loop(0, C, one, 0)
            pl.when(jnp.logical_and(block < r, r + 1 < R))(lambda: each("wait_send", pass_tiles(block, up())))
            pl.when(jnp.logical_and(block > r, r > 0))(lambda: each("wait_send", pass_tiles(block, down())))
        return carry

    lax.fori_loop(0, R, finish, 0)
    both_ways(lambda way, to: each("wait_send", own_tiles(way, to)))
    for dx, dk in order:
        both_ways(lambda way, to: own_piece(col_of(dx, dk), way, to, False).wait_send())
    for dx, dk in others:
        for ex, ek in order:
            s = col_of(ex, ek)
            from_other(dx, dk, s).wait_send()
        orb_to(dx, dk).wait_send()
        spread(dx, dk).wait_send()
    own.wait()


def product_kernel(pairs, orb, z, a, b, out, metric, upper, mixed):
    tiles = orb.shape[0] // 128
    n_local = z.shape[0] // pairs.shape[0]

    @pl.when(pl.program_id(0) == 0)
    def _():
        upper[...] = jnp.zeros_like(upper)

        def one(i, carry):
            block = i // n_local
            at = (i - block * n_local) * 2
            first = pairs[block, 0, at]
            second = pairs[block, 0, at + 1]
            offset = lax.rem(second - first + tiles, tiles)
            rows = orb[pl.ds(pl.multiple_of(first * 128, 128), 128), :]
            columns = orb[pl.ds(pl.multiple_of(second * 128, 128), 128), :]
            inter = lax.dot_general(rows, columns, (((1,), (1,)), ((), ())), preferred_element_type=jnp.float32)
            weight = (z[i].astype(jnp.float32) * inter).astype(jnp.bfloat16).astype(jnp.float32)
            slot = first * BAND + offset
            upper[slot] = upper[slot] + weight
            return carry

        lax.fori_loop(0, z.shape[0], one, 0, unroll=4)
        metric[...] = jnp.zeros_like(metric)
        for t in range(tiles):
            for offset in range(BAND):
                value = upper[t * BAND + offset]
                turned = value.T
                u = (t + offset) % tiles
                here, there = slice(t * 128, t * 128 + 128), slice(u * 128, u * 128 + 128)
                if offset == 0:
                    metric[here, here] = (value + turned).astype(jnp.bfloat16)
                else:
                    metric[here, there] = value.astype(jnp.bfloat16)
                    metric[there, here] = turned.astype(jnp.bfloat16)

    for u in range(0, tiles, 2):
        span = [(u - BAND + 1 + m) % tiles for m in range(2 * BAND)]
        runs = []
        for t in span:
            if runs and runs[-1][1] == t:
                runs[-1][1] = t + 1
            else:
                runs.append([t, t + 1])
        total = None
        for lo, hi in runs:
            term = jnp.dot(a[:, lo * 128:hi * 128], metric[lo * 128:hi * 128, u * 128:u * 128 + 256],
                           preferred_element_type=jnp.float32)
            total = term if total is None else total + term
        mixed[:, u * 128:u * 128 + 256] = total.astype(jnp.bfloat16)

    rows = a.shape[0]
    lines = b.shape[0] // 128
    step = next(s for s in (3, 2, 1) if lines % s == 0)

    for i in range(lines // step):
        value = lax.dot_general(mixed[...], b[i * step * 128:(i + 1) * step * 128, :],
                                (((1,), (1,)), ((), ())), preferred_element_type=jnp.float32)
        for q in range(step):
            out[pl.ds(i * step + q, rows, stride=lines), :] = value[:, q * 128:q * 128 + 128]


def on_device(dims, basis_values, orbital_values, z_tiles, tile_pairs):
    G, R, X, K = dims
    C = X * K
    block_rows, width = basis_values.shape
    S = block_rows // C
    points = width * C
    n_pair, tile, _ = z_tiles.shape
    orbs = orbital_values.shape[1]
    flat = tile_pairs.reshape(1, 2 * n_pair)
    flat = jnp.pad(flat, ((0, 7), (0, 128 - 2 * n_pair)))
    bf16 = jnp.bfloat16
    any_spec = pl.BlockSpec(memory_space=pl.ANY)
    dma = pltpu.SemaphoreType.DMA
    a_all, cols, orb_all, z_all, pairs_all = pl.pallas_call(
        functools.partial(gather_kernel, dims),
        out_shape=[
            jax.ShapeDtypeStruct((C, S, points), bf16),
            jax.ShapeDtypeStruct((R, S, points), bf16),
            jax.ShapeDtypeStruct((points, orbs), bf16),
            jax.ShapeDtypeStruct((R * n_pair, tile, tile), bf16),
            jax.ShapeDtypeStruct((R, 8, 128), jnp.int32),
        ],
        in_specs=[any_spec] * 4,
        out_specs=[any_spec] * 5,
        scratch_shapes=[
            dma((5,)), dma((X, K, C)), dma((X, K, C)), dma((X, K)), dma((X, K)),
            dma((R, C)), dma((2, C)), dma((R, C)),
            dma((G - 1, R, C)), dma((G - 1, R, C)),
            dma((R,)), dma((2,)), dma((R,)), dma((R,)), dma((2,)), dma((R,)),
            dma((X, K)), dma((X, K)),
        ],
        compiler_params=pltpu.CompilerParams(collective_id=0, has_side_effects=True),
    )(basis_values.reshape(C, S, width), orbital_values, z_tiles, flat)

    a = a_all.reshape(C * S, points)
    b = cols.reshape(R * S, points)
    lines = R * S // 128
    rows = next(m for m in range(384, 0, -16) if block_rows % m == 0)
    once = pl.Buffered(1)

    def whole(shape):
        return pl.BlockSpec(shape, lambda i: (0,) * len(shape), pipeline_mode=once)

    product = pl.pallas_call(
        product_kernel,
        grid=(block_rows // rows,),
        out_shape=jax.ShapeDtypeStruct((block_rows * lines, 128), jnp.float32),
        in_specs=[
            pl.BlockSpec(memory_space=pltpu.SMEM),
            whole((points, orbs)),
            whole((R * n_pair, tile, tile)),
            pl.BlockSpec((rows, points), lambda i: (i, 0)),
            whole((R * S, points)),
        ],
        out_specs=pl.BlockSpec((rows * lines, 128), lambda i: (i, 0)),
        scratch_shapes=[
            pltpu.VMEM((points, points), bf16),
            pltpu.VMEM((points // 128 * BAND, tile, tile), jnp.float32),
            pltpu.VMEM((rows, points), bf16),
        ],
        compiler_params=pltpu.CompilerParams(vmem_limit_bytes=56 * 1024 * 1024),
    )(pairs_all, orb_all, z_all, a, b)
    return product.reshape(block_rows, 1, R * S)


def solution(mesh):
    dims = tuple(mesh.shape[name] for name in ("groups", "row", "col", "rep"))
    placed = (
        P("row", ("col", "rep")),
        P(("groups", "col", "rep"), None),
        P("row", None, None),
        P("row", None),
    )
    return jax.shard_map(
        functools.partial(on_device, dims),
        mesh=mesh,
        in_specs=placed,
        out_specs=P(("groups", "row"), ("col", "rep"), None),
        check_vma=False,
    )
```

```python
import functools

import jax
import jax.numpy as jnp
from jax import lax
from jax.experimental import pallas as pl
from jax.experimental.pallas import tpu as pltpu
from jax.sharding import PartitionSpec as P

MESH = pl.DeviceIdType.MESH
BAND = 3


def gather_kernel(dims, basis, orb, z, pairs, a_all, cols, orb_all, z_all, pairs_all,
                  loc_sem, xs_sem, xr_sem, os_sem, or_sem, zs_sem, zo_sem, zr_sem,
                  ys_sem, yr_sem, ts_sem, to_sem, tr_sem, ps_sem, po_sem, pr_sem,
                  ds_sem, dr_sem, in_sem, held, held_orb, held_tiles, held_pairs, held_slice):
    G, R, X, K = dims
    C = X * K
    width = basis.shape[2]
    half = width // G
    n_pair = z.shape[0]
    part = z.shape[1] // C
    g = lax.axis_index("groups")
    r = lax.axis_index("row")
    x = lax.axis_index("col")
    k = lax.axis_index("rep")
    c = x * K + k

    def col_of(dx, dk):
        return lax.rem(x + dx, X) * K + lax.rem(k + dk, K)

    def dev(dg=0, row=None, dx=0, dk=0):
        return (lax.rem(g + dg, G), r if row is None else row, lax.rem(x + dx, X), lax.rem(k + dk, K))

    def remote(src, dst, send, recv, device):
        return pltpu.make_async_remote_copy(src_ref=src, dst_ref=dst, send_sem=send, recv_sem=recv,
                                            device_id=device, device_id_type=MESH)

    own_rows = z.at[:, pl.ds(pl.multiple_of(c * part, 16), part), :]
    staged = [
        pltpu.make_async_copy(basis, held, in_sem.at[0]),
        pltpu.make_async_copy(orb, held_orb, in_sem.at[1]),
        pltpu.make_async_copy(own_rows, held_tiles, in_sem.at[2]),
        pltpu.make_async_copy(pairs, held_pairs, in_sem.at[3]),
    ]
    for copy in staged:
        copy.start()

    others = [(dx, dk) for dx in range(X) for dk in range(K) if dx or dk]
    barrier = pltpu.get_barrier_semaphore()
    for dx, dk in others:
        pl.semaphore_signal(barrier, inc=1, device_id=dev(dx=dx, dk=dk), device_id_type=MESH)
    for dr in (1, R - 1):
        pl.semaphore_signal(barrier, inc=1, device_id=dev(row=lax.rem(r + dr, R)), device_id_type=MESH)
    for dg in range(1, G):
        pl.semaphore_signal(barrier, inc=1, device_id=dev(dg=dg), device_id_type=MESH)
    pl.semaphore_wait(barrier, len(others) + 2 + G - 1)

    def lanes(point_block):
        return pl.ds(pl.multiple_of(point_block * width, 128), width)

    def half_lanes(point_block, group):
        return pl.ds(pl.multiple_of(point_block * width + group * half, 128), half)

    def tile_rows(block):
        return z_all.at[pl.ds(block * n_pair, n_pair), pl.ds(pl.multiple_of(c * part, 16), part), :]

    def up():
        return dev(row=r + 1)

    def down():
        return dev(row=r - 1)

    def own_tiles(way, to):
        return (remote(own_rows, tile_rows(r), to_sem.at[way], tr_sem.at[r], to),
                remote(pairs, pairs_all.at[r], po_sem.at[way], pr_sem.at[r], to))

    def pass_tiles(block, to):
        return (remote(tile_rows(block), tile_rows(block), ts_sem.at[block], tr_sem.at[block], to),
                remote(pairs_all.at[block], pairs_all.at[block], ps_sem.at[block], pr_sem.at[block], to))

    def piece(block, point_block, group):
        return cols.at[block, :, half_lanes(point_block, group)]

    def own_piece(point_block, way, to, local):
        if local:
            src = basis.at[c, :, pl.ds(pl.multiple_of(g * half, 128), half)]
        else:
            src = a_all.at[c, :, half_lanes(point_block, g)]
        return remote(src, piece(r, point_block, g), zo_sem.at[way, point_block],
                      zr_sem.at[r, point_block], to)

    def pass_piece(block, point_block, to):
        ref = piece(block, point_block, g)
        return remote(ref, ref, zs_sem.at[block, point_block], zr_sem.at[block, point_block], to)

    def swap_piece(block, point_block, dg):
        ref = piece(block, point_block, g)
        return remote(ref, ref, ys_sem.at[dg - 1, block, point_block],
                      yr_sem.at[dg - 1, block, point_block], dev(dg=dg))

    def got_piece(block, point_block, dg):
        ref = piece(block, point_block, lax.rem(g + G - dg, G))
        return remote(ref, ref, ys_sem.at[dg - 1, block, point_block],
                      yr_sem.at[dg - 1, block, point_block], dev(dg=dg))

    def each(action, items):
        for item in items:
            getattr(item, action)()

    def both_ways(do):
        pl.when(r + 1 < R)(lambda: do(0, up()))
        pl.when(r > 0)(lambda: do(1, down()))

    def start_own(point_block, local=False):
        both_ways(lambda way, to: own_piece(point_block, way, to, local).start())

    both_ways(lambda way, to: each("start", own_tiles(way, to)))
    start_own(c, True)

    def to_core(dk, s):
        ref = a_all.at[s, :, lanes(c)]
        return remote(basis.at[s], ref, xs_sem.at[0, dk, s], xr_sem.at[0, dk, s], dev(dk=K - dk))

    def to_chip(dx, s):
        ref = a_all.at[s, :, lanes(c)]
        return remote(basis.at[s], ref, xs_sem.at[dx, 0, s], xr_sem.at[dx, 0, s], dev(dx=X - dx))

    def from_other(dx, dk, s):
        ref = a_all.at[s, :, lanes(col_of(dx, dk))]
        return remote(ref, ref, xs_sem.at[dx, dk, s], xr_sem.at[dx, dk, s], dev(dk=1))

    def hand_on(dx, dk, s):
        ref = a_all.at[s, :, lanes(col_of(dx, 0))]
        return remote(ref, ref, xs_sem.at[dx, dk, s], xr_sem.at[dx, dk, s], dev(dk=K - dk))

    own_orb = orb_all.at[pl.ds(pl.multiple_of(c * width, 16), width), :]

    def orb_to(dx, dk):
        return remote(orb, own_orb, os_sem.at[dx, dk], or_sem.at[dx, dk], dev(dx=lax.rem(X - dx, X), dk=lax.rem(K - dk, K)))

    def orb_from(dx, dk):
        ref = orb_all.at[pl.ds(pl.multiple_of(col_of(dx, dk) * width, 16), width), :]
        return remote(ref, ref, os_sem.at[dx, dk], or_sem.at[dx, dk], dev(dk=1))

    order = [(dx, dk) for dx in range(X) for dk in range(K)]
    for ex, ek in order:
        for dk in range(1, K):
            to_core(dk, lax.rem(x + ex, X) * K + lax.rem(k + K - dk + ek, K)).start()
        for dx in range(1, X):
            to_chip(dx, lax.rem(x + X - dx + ex, X) * K + lax.rem(k + ek, K)).start()
        if ex == 0 and ek == 0:
            for dx, dk in others:
                orb_to(dx, dk).start()

    local = [
        pltpu.make_async_copy(held, a_all.at[:, :, lanes(c)], loc_sem.at[0]),
        pltpu.make_async_copy(held_orb, own_orb, loc_sem.at[1]),
        pltpu.make_async_copy(held_tiles, tile_rows(r), loc_sem.at[2]),
        pltpu.make_async_copy(held_pairs, pairs_all.at[r], loc_sem.at[3]),
    ]
    for before, copy in zip(staged, local):
        before.wait()
        copy.start()

    for dk in range(1, K):
        from_other(0, dk, c).wait_recv()
        start_own(col_of(0, dk))

    def each_block(step, below, above):
        pl.when(r - step >= 0)(lambda: below(r - step))
        pl.when(r + step < R)(lambda: above(r + step))

    def relay_tiles(step, carry):
        def take(block, last, to):
            for t in pass_tiles(block, to):
                t.wait_recv()

            @pl.when(last)
            def _():
                for t in pass_tiles(block, to):
                    t.start()

        each_block(step, lambda b: take(b, r + 1 < R, up()), lambda b: take(b, r > 0, down()))
        return carry

    def relay(step, dxs):
        def take(block, point_block, more, to):
            pass_piece(block, point_block, to).wait_recv()
            pl.when(more)(lambda: pass_piece(block, point_block, to).start())
            for dg in range(1, G):
                swap_piece(block, point_block, dg).start()

        for dx in dxs:
            for dk in range(K):
                p = col_of(dx, dk)
                each_block(step, lambda b: take(b, p, r + 1 < R, up()), lambda b: take(b, p, r > 0, down()))

    lax.fori_loop(1, R, relay_tiles, 0)
    for copy in local[2:]:
        copy.wait()

    def all_rows(col):
        return z_all.at[:, pl.ds(pl.multiple_of(col * part, 16), part), :]

    def spread(dx, dk):
        return remote(all_rows(c), all_rows(c), ds_sem.at[dx, dk], dr_sem.at[dx, dk],
                      dev(dx=lax.rem(X - dx, X), dk=lax.rem(K - dk, K)))

    def spread_in(dx, dk):
        ref = all_rows(col_of(dx, dk))
        return remote(ref, ref, ds_sem.at[dx, dk], dr_sem.at[dx, dk], dev(dk=1))

    for dx, dk in others:
        spread(dx, dk).start()

    relay(1, [0])
    for dx in range(1, X):
        from_other(dx, 0, c).wait_recv()
        start_own(col_of(dx, 0))
    for dx in range(1, X):
        for dk in range(1, K):
            s = col_of(0, K - dk)
            from_other(dx, 0, s).wait_recv()
            hand_on(dx, dk, s).start()
    for dx in range(1, X):
        for dk in range(1, K):
            from_other(dx, dk, c).wait_recv()
            start_own(col_of(dx, dk))

    def first_part(step, carry):
        relay(step, [0])
        return carry

    def second_part(step, carry):
        relay(step, list(range(1, X)))
        return carry

    lax.fori_loop(2, R, first_part, 0)
    relay(1, list(range(1, X)))

    for dx in range(1, X):
        for ex, ek in order:
            if ex == 0 and ek < 1:
                for dk in range(1, K):
                    hand_on(dx, dk, c).start()
            elif ex:
                s = col_of(ex, ek)
                from_other(dx, 0, s).wait_recv()
                for dk in range(1, K):
                    hand_on(dx, dk, s).start()
            else:
                s = col_of(0, ek)
                for dk in range(1, K):
                    if K - dk != ek:
                        hand_on(dx, dk, s).start()

    lax.fori_loop(2, R, second_part, 0)

    for dx, dk in others:
        for ex, ek in order:
            if ex == 0 and ek == 0:
                continue
            if dk == 0 and dx:
                continue
            from_other(dx, dk, col_of(ex, ek)).wait_recv()
        orb_from(dx, dk).wait_recv()
        spread_in(dx, dk).wait_recv()
    local[0].wait()
    local[1].wait()
    take = pltpu.make_async_copy(a_all.at[c], held_slice, in_sem.at[4])
    take.start()
    take.wait()
    own = pltpu.make_async_copy(held_slice, cols.at[r], loc_sem.at[4])
    own.start()

    def finish(block, carry):
        @pl.when(block != r)
        def _():
            def one(p, inner):
                for dg in range(1, G):
                    got_piece(block, p, dg).wait_recv()
                    swap_piece(block, p, dg).wait_send()
                pl.when(jnp.logical_and(block < r, r + 1 < R))(lambda: pass_piece(block, p, up()).wait_send())
                pl.when(jnp.logical_and(block > r, r > 0))(lambda: pass_piece(block, p, down()).wait_send())
                return inner

            lax.fori_loop(0, C, one, 0)
            pl.when(jnp.logical_and(block < r, r + 1 < R))(lambda: each("wait_send", pass_tiles(block, up())))
            pl.when(jnp.logical_and(block > r, r > 0))(lambda: each("wait_send", pass_tiles(block, down())))
        return carry

    lax.fori_loop(0, R, finish, 0)
    both_ways(lambda way, to: each("wait_send", own_tiles(way, to)))
    for dx, dk in order:
        both_ways(lambda way, to: own_piece(col_of(dx, dk), way, to, False).wait_send())
    for dx, dk in others:
        for ex, ek in order:
            s = col_of(ex, ek)
            from_other(dx, dk, s).wait_send()
        orb_to(dx, dk).wait_send()
        spread(dx, dk).wait_send()
    own.wait()


def product_kernel(pairs, orb, z, a, b, out, metric, upper, mixed):
    tiles = orb.shape[0] // 128
    n_local = z.shape[0] // pairs.shape[0]

    @pl.when(pl.program_id(0) == 0)
    def _():
        upper[...] = jnp.zeros_like(upper)

        def one(i, carry):
            block = i // n_local
            at = (i - block * n_local) * 2
            first = pairs[block, 0, at]
            second = pairs[block, 0, at + 1]
            offset = lax.rem(second - first + tiles, tiles)
            rows = orb[pl.ds(pl.multiple_of(first * 128, 128), 128), :]
            columns = orb[pl.ds(pl.multiple_of(second * 128, 128), 128), :]
            inter = lax.dot_general(rows, columns, (((1,), (1,)), ((), ())), preferred_element_type=jnp.float32)
            weight = (z[i].astype(jnp.float32) * inter).astype(jnp.bfloat16).astype(jnp.float32)
            slot = first * BAND + offset
            upper[slot] = upper[slot] + weight
            return carry

        lax.fori_loop(0, z.shape[0], one, 0, unroll=4)
        metric[...] = jnp.zeros_like(metric)
        for t in range(tiles):
            for offset in range(BAND):
                value = upper[t * BAND + offset]
                turned = value.T
                u = (t + offset) % tiles
                here, there = slice(t * 128, t * 128 + 128), slice(u * 128, u * 128 + 128)
                if offset == 0:
                    metric[here, here] = (value + turned).astype(jnp.bfloat16)
                else:
                    metric[here, there] = value.astype(jnp.bfloat16)
                    metric[there, here] = turned.astype(jnp.bfloat16)

    for u in range(0, tiles, 2):
        span = [(u - BAND + 1 + m) % tiles for m in range(2 * BAND)]
        runs = []
        for t in span:
            if runs and runs[-1][1] == t:
                runs[-1][1] = t + 1
            else:
                runs.append([t, t + 1])
        total = None
        for lo, hi in runs:
            term = jnp.dot(a[:, lo * 128:hi * 128], metric[lo * 128:hi * 128, u * 128:u * 128 + 256],
                           preferred_element_type=jnp.float32)
            total = term if total is None else total + term
        mixed[:, u * 128:u * 128 + 256] = total.astype(jnp.bfloat16)

    rows = a.shape[0]
    lines = b.shape[0] // 128
    step = next(s for s in (3, 2, 1) if lines % s == 0)

    for i in range(lines // step):
        value = lax.dot_general(mixed[...], b[i * step * 128:(i + 1) * step * 128, :],
                                (((1,), (1,)), ((), ())), preferred_element_type=jnp.float32)
        for q in range(step):
            out[pl.ds(i * step + q, rows, stride=lines), :] = value[:, q * 128:q * 128 + 128]


def on_device(dims, basis_values, orbital_values, z_tiles, tile_pairs):
    G, R, X, K = dims
    C = X * K
    block_rows, width = basis_values.shape
    S = block_rows // C
    points = width * C
    n_pair, tile, _ = z_tiles.shape
    orbs = orbital_values.shape[1]
    flat = tile_pairs.reshape(1, 2 * n_pair)
    flat = jnp.pad(flat, ((0, 7), (0, 128 - 2 * n_pair)))
    bf16 = jnp.bfloat16
    any_spec = pl.BlockSpec(memory_space=pl.ANY)
    dma = pltpu.SemaphoreType.DMA
    a_all, cols, orb_all, z_all, pairs_all = pl.pallas_call(
        functools.partial(gather_kernel, dims),
        out_shape=[
            jax.ShapeDtypeStruct((C, S, points), bf16),
            jax.ShapeDtypeStruct((R, S, points), bf16),
            jax.ShapeDtypeStruct((points, orbs), bf16),
            jax.ShapeDtypeStruct((R * n_pair, tile, tile), bf16),
            jax.ShapeDtypeStruct((R, 8, 128), jnp.int32),
        ],
        in_specs=[any_spec] * 4,
        out_specs=[any_spec] * 5,
        scratch_shapes=[
            dma((5,)), dma((X, K, C)), dma((X, K, C)), dma((X, K)), dma((X, K)),
            dma((R, C)), dma((2, C)), dma((R, C)),
            dma((G - 1, R, C)), dma((G - 1, R, C)),
            dma((R,)), dma((2,)), dma((R,)), dma((R,)), dma((2,)), dma((R,)),
            dma((X, K)), dma((X, K)), dma((5,)),
            pltpu.VMEM((C, S, width), bf16),
            pltpu.VMEM((width, orbs), bf16),
            pltpu.VMEM((n_pair, tile // C, tile), bf16),
            pltpu.VMEM((8, 128), jnp.int32),
            pltpu.VMEM((S, points), bf16),
        ],
        compiler_params=pltpu.CompilerParams(
            collective_id=0, has_side_effects=True, vmem_limit_bytes=40 * 1024 * 1024
        ),
    )(basis_values.reshape(C, S, width), orbital_values, z_tiles, flat)

    a = a_all.reshape(C * S, points)
    b = cols.reshape(R * S, points)
    lines = R * S // 128
    rows = next(m for m in range(384, 0, -16) if block_rows % m == 0)
    once = pl.Buffered(1)

    def whole(shape):
        return pl.BlockSpec(shape, lambda i: (0,) * len(shape), pipeline_mode=once)

    product = pl.pallas_call(
        product_kernel,
        grid=(block_rows // rows,),
        out_shape=jax.ShapeDtypeStruct((block_rows * lines, 128), jnp.float32),
        in_specs=[
            pl.BlockSpec(memory_space=pltpu.SMEM),
            whole((points, orbs)),
            whole((R * n_pair, tile, tile)),
            pl.BlockSpec((rows, points), lambda i: (i, 0)),
            whole((R * S, points)),
        ],
        out_specs=pl.BlockSpec((rows * lines, 128), lambda i: (i, 0)),
        scratch_shapes=[
            pltpu.VMEM((points, points), bf16),
            pltpu.VMEM((points // 128 * BAND, tile, tile), jnp.float32),
            pltpu.VMEM((rows, points), bf16),
        ],
        compiler_params=pltpu.CompilerParams(vmem_limit_bytes=56 * 1024 * 1024),
    )(pairs_all, orb_all, z_all, a, b)
    return product.reshape(block_rows, 1, R * S)


def solution(mesh):
    dims = tuple(mesh.shape[name] for name in ("groups", "row", "col", "rep"))
    placed = (
        P("row", ("col", "rep")),
        P(("groups", "col", "rep"), None),
        P("row", None, None),
        P("row", None),
    )
    return jax.shard_map(
        functools.partial(on_device, dims),
        mesh=mesh,
        in_specs=placed,
        out_specs=P(("groups", "row"), ("col", "rep"), None),
        check_vma=False,
    )
```

```python
import functools

import jax
import jax.numpy as jnp
from jax import lax
from jax.experimental import pallas as pl
from jax.experimental.pallas import tpu as pltpu
from jax.sharding import PartitionSpec as P

MESH = pl.DeviceIdType.MESH
BAND = 3


def gather_kernel(dims, basis, orb, z, pairs, a_all, cols, orb_all, z_all, pairs_all,
                  loc_sem, xs_sem, xr_sem, os_sem, or_sem, zs_sem, zo_sem, zr_sem,
                  ys_sem, yr_sem, ts_sem, to_sem, tr_sem, ps_sem, po_sem, pr_sem,
                  ds_sem, dr_sem, in_sem, held, held_orb, held_tiles, held_pairs, held_slice):
    G, R, X, K = dims
    C = X * K
    width = basis.shape[2]
    half = width // G
    n_pair = z.shape[0]
    part = z.shape[1] // C
    g = lax.axis_index("groups")
    r = lax.axis_index("row")
    x = lax.axis_index("col")
    k = lax.axis_index("rep")
    c = x * K + k

    def col_of(dx, dk):
        return lax.rem(x + dx, X) * K + lax.rem(k + dk, K)

    def dev(dg=0, row=None, dx=0, dk=0):
        return (lax.rem(g + dg, G), r if row is None else row, lax.rem(x + dx, X), lax.rem(k + dk, K))

    def remote(src, dst, send, recv, device):
        return pltpu.make_async_remote_copy(src_ref=src, dst_ref=dst, send_sem=send, recv_sem=recv,
                                            device_id=device, device_id_type=MESH)

    own_rows = z.at[:, pl.ds(pl.multiple_of(c * part, 16), part), :]
    staged = [
        pltpu.make_async_copy(basis, held, in_sem.at[0]),
        pltpu.make_async_copy(orb, held_orb, in_sem.at[1]),
        pltpu.make_async_copy(own_rows, held_tiles, in_sem.at[2]),
        pltpu.make_async_copy(pairs, held_pairs, in_sem.at[3]),
    ]
    for copy in staged:
        copy.start()

    others = [(dx, dk) for dx in range(X) for dk in range(K) if dx or dk]
    barrier = pltpu.get_barrier_semaphore()
    for dx, dk in others:
        pl.semaphore_signal(barrier, inc=1, device_id=dev(dx=dx, dk=dk), device_id_type=MESH)
    for dr in (1, R - 1):
        pl.semaphore_signal(barrier, inc=1, device_id=dev(row=lax.rem(r + dr, R)), device_id_type=MESH)
    for dg in range(1, G):
        pl.semaphore_signal(barrier, inc=1, device_id=dev(dg=dg), device_id_type=MESH)
    pl.semaphore_wait(barrier, len(others) + 2 + G - 1)

    def lanes(point_block):
        return pl.ds(pl.multiple_of(point_block * width, 128), width)

    def half_lanes(point_block, group):
        return pl.ds(pl.multiple_of(point_block * width + group * half, 128), half)

    def tile_rows(block):
        return z_all.at[pl.ds(block * n_pair, n_pair), pl.ds(pl.multiple_of(c * part, 16), part), :]

    def up():
        return dev(row=r + 1)

    def down():
        return dev(row=r - 1)

    def own_tiles(way, to):
        return (remote(own_rows, tile_rows(r), to_sem.at[way], tr_sem.at[r], to),
                remote(pairs, pairs_all.at[r], po_sem.at[way], pr_sem.at[r], to))

    def pass_tiles(block, to):
        return (remote(tile_rows(block), tile_rows(block), ts_sem.at[block], tr_sem.at[block], to),
                remote(pairs_all.at[block], pairs_all.at[block], ps_sem.at[block], pr_sem.at[block], to))

    def piece(block, point_block, group):
        return cols.at[block, :, half_lanes(point_block, group)]

    def own_piece(point_block, way, to, local):
        if local:
            src = basis.at[c, :, pl.ds(pl.multiple_of(g * half, 128), half)]
        else:
            src = a_all.at[c, :, half_lanes(point_block, g)]
        return remote(src, piece(r, point_block, g), zo_sem.at[way, point_block],
                      zr_sem.at[r, point_block], to)

    def pass_piece(block, point_block, to):
        ref = piece(block, point_block, g)
        return remote(ref, ref, zs_sem.at[block, point_block], zr_sem.at[block, point_block], to)

    def swap_piece(block, point_block, dg):
        ref = piece(block, point_block, g)
        return remote(ref, ref, ys_sem.at[dg - 1, block, point_block],
                      yr_sem.at[dg - 1, block, point_block], dev(dg=dg))

    def got_piece(block, point_block, dg):
        ref = piece(block, point_block, lax.rem(g + G - dg, G))
        return remote(ref, ref, ys_sem.at[dg - 1, block, point_block],
                      yr_sem.at[dg - 1, block, point_block], dev(dg=dg))

    def each(action, items):
        for item in items:
            getattr(item, action)()

    def both_ways(do):
        pl.when(r + 1 < R)(lambda: do(0, up()))
        pl.when(r > 0)(lambda: do(1, down()))

    def start_own(point_block, local=False):
        both_ways(lambda way, to: own_piece(point_block, way, to, local).start())

    both_ways(lambda way, to: each("start", own_tiles(way, to)))
    start_own(c, True)

    def to_core(dk, s):
        ref = a_all.at[s, :, lanes(c)]
        return remote(basis.at[s], ref, xs_sem.at[0, dk, s], xr_sem.at[0, dk, s], dev(dk=K - dk))

    def to_chip(dx, s):
        ref = a_all.at[s, :, lanes(c)]
        return remote(basis.at[s], ref, xs_sem.at[dx, 0, s], xr_sem.at[dx, 0, s], dev(dx=X - dx))

    def from_other(dx, dk, s):
        ref = a_all.at[s, :, lanes(col_of(dx, dk))]
        return remote(ref, ref, xs_sem.at[dx, dk, s], xr_sem.at[dx, dk, s], dev(dk=1))

    def hand_on(dx, dk, s):
        ref = a_all.at[s, :, lanes(col_of(dx, 0))]
        return remote(ref, ref, xs_sem.at[dx, dk, s], xr_sem.at[dx, dk, s], dev(dk=K - dk))

    own_orb = orb_all.at[pl.ds(pl.multiple_of(c * width, 16), width), :]

    def orb_to(dx, dk):
        return remote(orb, own_orb, os_sem.at[dx, dk], or_sem.at[dx, dk], dev(dx=lax.rem(X - dx, X), dk=lax.rem(K - dk, K)))

    def orb_from(dx, dk):
        ref = orb_all.at[pl.ds(pl.multiple_of(col_of(dx, dk) * width, 16), width), :]
        return remote(ref, ref, os_sem.at[dx, dk], or_sem.at[dx, dk], dev(dk=1))

    order = [(dx, dk) for dx in range(X) for dk in range(K)]
    def send_slices(ex, ek):
        for dk in range(1, K):
            to_core(dk, lax.rem(x + ex, X) * K + lax.rem(k + K - dk + ek, K)).start()
        for dx in range(1, X):
            to_chip(dx, lax.rem(x + X - dx + ex, X) * K + lax.rem(k + ek, K)).start()

    for ek in range(K):
        send_slices(0, ek)

    local = [
        pltpu.make_async_copy(held, a_all.at[:, :, lanes(c)], loc_sem.at[0]),
        pltpu.make_async_copy(held_orb, own_orb, loc_sem.at[1]),
        pltpu.make_async_copy(held_tiles, tile_rows(r), loc_sem.at[2]),
        pltpu.make_async_copy(held_pairs, pairs_all.at[r], loc_sem.at[3]),
    ]
    for before, copy in zip(staged, local):
        before.wait()
        copy.start()

    for dk in range(1, K):
        from_other(0, dk, c).wait_recv()
        start_own(col_of(0, dk))

    def each_block(step, below, above):
        pl.when(r - step >= 0)(lambda: below(r - step))
        pl.when(r + step < R)(lambda: above(r + step))

    def relay_tiles(step, carry):
        def take(block, last, to):
            for t in pass_tiles(block, to):
                t.wait_recv()

            @pl.when(last)
            def _():
                for t in pass_tiles(block, to):
                    t.start()

        each_block(step, lambda b: take(b, r + 1 < R, up()), lambda b: take(b, r > 0, down()))
        return carry

    def relay(step, dxs):
        def take(block, point_block, more, to):
            pass_piece(block, point_block, to).wait_recv()
            pl.when(more)(lambda: pass_piece(block, point_block, to).start())
            for dg in range(1, G):
                swap_piece(block, point_block, dg).start()

        for dx in dxs:
            for dk in range(K):
                p = col_of(dx, dk)
                each_block(step, lambda b: take(b, p, r + 1 < R, up()), lambda b: take(b, p, r > 0, down()))

    lax.fori_loop(1, R, relay_tiles, 0)
    for copy in local[2:]:
        copy.wait()

    def all_rows(col):
        return z_all.at[:, pl.ds(pl.multiple_of(col * part, 16), part), :]

    def spread(dx, dk):
        return remote(all_rows(c), all_rows(c), ds_sem.at[dx, dk], dr_sem.at[dx, dk],
                      dev(dx=lax.rem(X - dx, X), dk=lax.rem(K - dk, K)))

    def spread_in(dx, dk):
        ref = all_rows(col_of(dx, dk))
        return remote(ref, ref, ds_sem.at[dx, dk], dr_sem.at[dx, dk], dev(dk=1))

    relay(1, [0])
    for dx in range(1, X):
        from_other(dx, 0, c).wait_recv()
        start_own(col_of(dx, 0))
    for dx in range(1, X):
        for dk in range(1, K):
            s = col_of(0, K - dk)
            from_other(dx, 0, s).wait_recv()
            hand_on(dx, dk, s).start()
    for ex in range(1, X):
        for ek in range(K):
            send_slices(ex, ek)
    for dx, dk in others:
        orb_to(dx, dk).start()
    for dx in range(1, X):
        for dk in range(1, K):
            from_other(dx, dk, c).wait_recv()
            start_own(col_of(dx, dk))

    def first_part(step, carry):
        relay(step, [0])
        return carry

    def second_part(step, carry):
        relay(step, list(range(1, X)))
        return carry

    lax.fori_loop(2, R, first_part, 0)
    relay(1, list(range(1, X)))

    for dx, dk in others:
        spread(dx, dk).start()

    for dx in range(1, X):
        for ex, ek in order:
            if ex == 0 and ek < 1:
                for dk in range(1, K):
                    hand_on(dx, dk, c).start()
            elif ex:
                s = col_of(ex, ek)
                from_other(dx, 0, s).wait_recv()
                for dk in range(1, K):
                    hand_on(dx, dk, s).start()
            else:
                s = col_of(0, ek)
                for dk in range(1, K):
                    if K - dk != ek:
                        hand_on(dx, dk, s).start()

    lax.fori_loop(2, R, second_part, 0)

    for dx, dk in others:
        for ex, ek in order:
            if ex == 0 and ek == 0:
                continue
            if dk == 0 and dx:
                continue
            from_other(dx, dk, col_of(ex, ek)).wait_recv()
        orb_from(dx, dk).wait_recv()
        spread_in(dx, dk).wait_recv()
    local[0].wait()
    local[1].wait()
    take = pltpu.make_async_copy(a_all.at[c], held_slice, in_sem.at[4])
    take.start()
    take.wait()
    own = pltpu.make_async_copy(held_slice, cols.at[r], loc_sem.at[4])
    own.start()

    def finish(block, carry):
        @pl.when(block != r)
        def _():
            def one(p, inner):
                for dg in range(1, G):
                    got_piece(block, p, dg).wait_recv()
                    swap_piece(block, p, dg).wait_send()
                pl.when(jnp.logical_and(block < r, r + 1 < R))(lambda: pass_piece(block, p, up()).wait_send())
                pl.when(jnp.logical_and(block > r, r > 0))(lambda: pass_piece(block, p, down()).wait_send())
                return inner

            lax.fori_loop(0, C, one, 0)
            pl.when(jnp.logical_and(block < r, r + 1 < R))(lambda: each("wait_send", pass_tiles(block, up())))
            pl.when(jnp.logical_and(block > r, r > 0))(lambda: each("wait_send", pass_tiles(block, down())))
        return carry

    lax.fori_loop(0, R, finish, 0)
    both_ways(lambda way, to: each("wait_send", own_tiles(way, to)))
    for dx, dk in order:
        both_ways(lambda way, to: own_piece(col_of(dx, dk), way, to, False).wait_send())
    for dx, dk in others:
        for ex, ek in order:
            s = col_of(ex, ek)
            from_other(dx, dk, s).wait_send()
        orb_to(dx, dk).wait_send()
        spread(dx, dk).wait_send()
    own.wait()


def product_kernel(pairs, orb, z, a, b, out, metric, upper, mixed):
    tiles = orb.shape[0] // 128
    n_local = z.shape[0] // pairs.shape[0]

    @pl.when(pl.program_id(0) == 0)
    def _():
        upper[...] = jnp.zeros_like(upper)

        def one(i, carry):
            block = i // n_local
            at = (i - block * n_local) * 2
            first = pairs[block, 0, at]
            second = pairs[block, 0, at + 1]
            offset = lax.rem(second - first + tiles, tiles)
            rows = orb[pl.ds(pl.multiple_of(first * 128, 128), 128), :]
            columns = orb[pl.ds(pl.multiple_of(second * 128, 128), 128), :]
            inter = lax.dot_general(rows, columns, (((1,), (1,)), ((), ())), preferred_element_type=jnp.float32)
            weight = (z[i].astype(jnp.float32) * inter).astype(jnp.bfloat16).astype(jnp.float32)
            slot = first * BAND + offset
            upper[slot] = upper[slot] + weight
            return carry

        lax.fori_loop(0, z.shape[0], one, 0, unroll=4)
        metric[...] = jnp.zeros_like(metric)
        for t in range(tiles):
            for offset in range(BAND):
                value = upper[t * BAND + offset]
                turned = value.T
                u = (t + offset) % tiles
                here, there = slice(t * 128, t * 128 + 128), slice(u * 128, u * 128 + 128)
                if offset == 0:
                    metric[here, here] = (value + turned).astype(jnp.bfloat16)
                else:
                    metric[here, there] = value.astype(jnp.bfloat16)
                    metric[there, here] = turned.astype(jnp.bfloat16)

    for u in range(0, tiles, 2):
        span = [(u - BAND + 1 + m) % tiles for m in range(2 * BAND)]
        runs = []
        for t in span:
            if runs and runs[-1][1] == t:
                runs[-1][1] = t + 1
            else:
                runs.append([t, t + 1])
        total = None
        for lo, hi in runs:
            term = jnp.dot(a[:, lo * 128:hi * 128], metric[lo * 128:hi * 128, u * 128:u * 128 + 256],
                           preferred_element_type=jnp.float32)
            total = term if total is None else total + term
        mixed[:, u * 128:u * 128 + 256] = total.astype(jnp.bfloat16)

    rows = a.shape[0]
    lines = b.shape[0] // 128
    step = next(s for s in (3, 2, 1) if lines % s == 0)

    for i in range(lines // step):
        value = lax.dot_general(mixed[...], b[i * step * 128:(i + 1) * step * 128, :],
                                (((1,), (1,)), ((), ())), preferred_element_type=jnp.float32)
        for q in range(step):
            out[pl.ds(i * step + q, rows, stride=lines), :] = value[:, q * 128:q * 128 + 128]


def on_device(dims, basis_values, orbital_values, z_tiles, tile_pairs):
    G, R, X, K = dims
    C = X * K
    block_rows, width = basis_values.shape
    S = block_rows // C
    points = width * C
    n_pair, tile, _ = z_tiles.shape
    orbs = orbital_values.shape[1]
    flat = tile_pairs.reshape(1, 2 * n_pair)
    flat = jnp.pad(flat, ((0, 7), (0, 128 - 2 * n_pair)))
    bf16 = jnp.bfloat16
    any_spec = pl.BlockSpec(memory_space=pl.ANY)
    dma = pltpu.SemaphoreType.DMA
    a_all, cols, orb_all, z_all, pairs_all = pl.pallas_call(
        functools.partial(gather_kernel, dims),
        out_shape=[
            jax.ShapeDtypeStruct((C, S, points), bf16),
            jax.ShapeDtypeStruct((R, S, points), bf16),
            jax.ShapeDtypeStruct((points, orbs), bf16),
            jax.ShapeDtypeStruct((R * n_pair, tile, tile), bf16),
            jax.ShapeDtypeStruct((R, 8, 128), jnp.int32),
        ],
        in_specs=[any_spec] * 4,
        out_specs=[any_spec] * 5,
        scratch_shapes=[
            dma((5,)), dma((X, K, C)), dma((X, K, C)), dma((X, K)), dma((X, K)),
            dma((R, C)), dma((2, C)), dma((R, C)),
            dma((G - 1, R, C)), dma((G - 1, R, C)),
            dma((R,)), dma((2,)), dma((R,)), dma((R,)), dma((2,)), dma((R,)),
            dma((X, K)), dma((X, K)), dma((5,)),
            pltpu.VMEM((C, S, width), bf16),
            pltpu.VMEM((width, orbs), bf16),
            pltpu.VMEM((n_pair, tile // C, tile), bf16),
            pltpu.VMEM((8, 128), jnp.int32),
            pltpu.VMEM((S, points), bf16),
        ],
        compiler_params=pltpu.CompilerParams(
            collective_id=0, has_side_effects=True, vmem_limit_bytes=60 * 1024 * 1024
        ),
    )(basis_values.reshape(C, S, width), orbital_values, z_tiles, flat)

    a = a_all.reshape(C * S, points)
    b = cols.reshape(R * S, points)
    lines = R * S // 128
    rows = next(m for m in range(384, 0, -16) if block_rows % m == 0)
    once = pl.Buffered(1)

    def whole(shape):
        return pl.BlockSpec(shape, lambda i: (0,) * len(shape), pipeline_mode=once)

    product = pl.pallas_call(
        product_kernel,
        grid=(block_rows // rows,),
        out_shape=jax.ShapeDtypeStruct((block_rows * lines, 128), jnp.float32),
        in_specs=[
            pl.BlockSpec(memory_space=pltpu.SMEM),
            whole((points, orbs)),
            whole((R * n_pair, tile, tile)),
            pl.BlockSpec((rows, points), lambda i: (i, 0)),
            whole((R * S, points)),
        ],
        out_specs=pl.BlockSpec((rows * lines, 128), lambda i: (i, 0)),
        scratch_shapes=[
            pltpu.VMEM((points, points), bf16),
            pltpu.VMEM((points // 128 * BAND, tile, tile), jnp.float32),
            pltpu.VMEM((rows, points), bf16),
        ],
        compiler_params=pltpu.CompilerParams(vmem_limit_bytes=56 * 1024 * 1024),
    )(pairs_all, orb_all, z_all, a, b)
    return product.reshape(block_rows, 1, R * S)


def solution(mesh):
    dims = tuple(mesh.shape[name] for name in ("groups", "row", "col", "rep"))
    placed = (
        P("row", ("col", "rep")),
        P(("groups", "col", "rep"), None),
        P("row", None, None),
        P("row", None),
    )
    return jax.shard_map(
        functools.partial(on_device, dims),
        mesh=mesh,
        in_specs=placed,
        out_specs=P(("groups", "row"), ("col", "rep"), None),
        check_vma=False,
    )
```
